512 devices in a mesh: sta: 8 (over x, core), tm: 32 (over y, z_hi), tpl: 2 (over z_lo).
Axes of the slice: x: 4, y: 8, z: 8 (z_hi: 4, z_lo: 2; z = z_hi * 2 + z_lo), core: 2. Of those that a mesh axis runs over, the one named last changes fastest.
Arguments:
- waveforms: bfloat16 [8, 32768], P('sta', 'tm'), may hold values from -120 to 120
- templates: bfloat16 [512, 300], P('tpl'), may hold values from -0.375 to 0.375
- moveouts: int32 [8, 512], P('sta', 'tpl'), may hold values from 0 to 719
- channel_mask: int32 [8, 512], P('sta', 'tpl'), may hold values 0 or 1
Outputs:
- stack: bfloat16 [512, 32768], P('tpl', 'tm')
The draws below stay inside these ranges and needn't reach their ends.
All inputs are finite; a program needn't handle non-finite values. No bound on the sum of `channel_mask` on one device may be relied on, other than what follows from the above.
Results may differ from the reference program's by a relative error of at most 0.015.
Values may be sent and summed in bfloat16 or wider, within the bound.
No kernel may reach another device: no remote copies, remote signals or barrier semaphores. Data moves between devices by JAX's collectives and lax.ppermute only.
A program may use at most 64 MiB of HBM per device.

```python
import math
import jax
import jax.numpy as jnp
from jax import lax

STA_DEV = 1
L = 300
TEMPLATES = 512
MOVE = 720
STATIONS = 8
TIMES = 32768
N_STA = 8


def draw_waveforms(key, part):
    key = jax.random.fold_in(key, 11)
    key_noise, key_station, key_segment, key_sample = jax.random.split(key, 4)
    noise = jnp.clip(jax.random.normal(key_noise, (STATIONS, TIMES), jnp.float32), -4.0, 4.0)
    station_gain = jnp.exp(jax.random.uniform(key_station, (STATIONS, 1), jnp.float32, -math.log(3.0), math.log(3.0)))
    segment_table = jnp.exp(jax.random.uniform(key_segment, (STATIONS, TIMES // 64), jnp.float32, -math.log(3.0), math.log(3.0)))
    segment_gain = jnp.repeat(segment_table, 64, axis=1)
    sample_gain = jnp.exp(jax.random.uniform(key_sample, (STATIONS, TIMES), jnp.float32, -math.log(2.0), math.log(2.0)))
    return (noise * station_gain * segment_gain * sample_gain).astype(jnp.bfloat16)


def set_ends(entries, key, smallest, top_value):
    longest = entries.shape.index(max(entries.shape))
    spots = []
    for shift in (0, 1):
        where = [jax.random.randint(jax.random.fold_in(key, axis), (), 0, length) for axis, length in enumerate(entries.shape)]
        where[longest] = (where[longest] + shift) % entries.shape[longest]
        spots.append(tuple(where))
    return entries.at[spots[0]].set(smallest).at[spots[1]].set(top_value)


def block_levels(rng, dims, shards, low, high):
    def one(dim, parts):
        heights = jax.random.uniform(jax.random.fold_in(jax.random.fold_in(rng, 6), dim), (parts,), jnp.float32, low / len(shards), high / len(shards))
        return jnp.repeat(jnp.exp(heights), dims[dim] // parts).reshape((-1,) + (1,) * (len(dims) - dim - 1))

    gain = one(*shards[0])
    for cut in shards[1:]:
        gain = gain * one(*cut)
    return gain


def centred(stream_key, dims, deviation, bound, shards=(), held_as=jnp.bfloat16):
    entries = jax.random.normal(stream_key, dims, jnp.float32) * deviation
    if len(shards) > 0:
        entries = block_levels(stream_key, dims, shards, -0.22, 0.18) * entries
    return jnp.clip(entries, min=-bound, max=bound).astype(held_as)


def setup_inputs(seed: int = 0) -> dict:
    splits = jax.random.split(jax.random.key(seed), 5)
    return {
        "waveforms": draw_waveforms(jax.random.fold_in(splits[4], 71), 0),
        "templates": centred(splits[1], (TEMPLATES, L), L ** -0.5, 0.375, ((0, 2),)),
        "moveouts": set_ends(jax.random.randint(splits[2], (STATIONS, TEMPLATES), 0, MOVE), jax.random.fold_in(splits[2], 1), 0, MOVE - 1).astype(jnp.int32),
        "channel_mask": set_ends((jax.random.randint(splits[3], (STATIONS, TEMPLATES), 0, 4) < 3).astype(jnp.int32), jax.random.fold_in(splits[3], 1), 0, 1),
    }


epsilon = 1e-05

def station_terms(samples, bank, window_len, template_len):
    window_index = jnp.arange(window_len)[:, None] + jnp.arange(template_len)[None, :]
    toeplitz = samples[window_index].astype(jnp.float32)
    correlated = jnp.dot(bank.astype(jnp.float32), toeplitz.T, precision=lax.Precision.HIGHEST, preferred_element_type=jnp.float32)
    squares = jnp.square(samples.astype(jnp.float32))
    energy = lax.reduce_window(squares, jnp.zeros((), squares.dtype), lax.add, (template_len,), (1,), 'VALID')
    return correlated * lax.rsqrt(energy / template_len + epsilon)[None, :]

def reference(waveforms, templates, moveouts, channel_mask):
    padded = jnp.pad(waveforms, ((0, 0), (0, MOVE + L - 1)))
    weight_scale = 1.0 / math.sqrt(STATIONS)
    shift_index = jnp.arange(TIMES, dtype=jnp.int32)[None, :]

    def station_step(running, station_item):
        samples, moves_row, mask_row = station_item
        normed = station_terms(samples, templates, TIMES + MOVE, L)
        picked = jnp.take_along_axis(normed, shift_index + moves_row[:, None], axis=1)
        return (running + (mask_row.astype(jnp.float32) * weight_scale)[:, None] * picked, None)

    def group_step(summed, group_item):
        partial_sum, unused = lax.scan(station_step, jnp.zeros((TEMPLATES, TIMES), jnp.float32), group_item)
        rounded = lax.optimization_barrier(partial_sum.astype(jnp.bfloat16))
        return (summed + rounded.astype(jnp.float32), None)
    group_items = (padded.reshape(N_STA, STA_DEV, TIMES + MOVE + L - 1), moveouts.reshape(N_STA, STA_DEV, TEMPLATES), channel_mask.reshape(N_STA, STA_DEV, TEMPLATES))
    summed, unused = lax.scan(group_step, jnp.zeros((TEMPLATES, TIMES), jnp.float32), group_items)
    return summed.astype(jnp.bfloat16)
```

```python
import functools
import math

import jax
import jax.numpy as jnp
from jax import lax
from jax.experimental import pallas as pl
from jax.experimental.pallas import tpu as pltpu
from jax.sharding import PartitionSpec as P

MOVE = 720
EPSILON = 1e-05
LANES = 128
ROW_STEP = 17


def rolled_left(x, by):
    return x if by == 0 else pltpu.roll(x, x.shape[1] - by, 1)


def pack_kernel(wave_ref, moves_ref, mask_ref, out_ref):
    moves = moves_ref[...]
    fields = (wave_ref[...].astype(jnp.float32), moves >> 7, moves & 127, mask_ref[...])
    line = jnp.concatenate([field.astype(jnp.float32) for field in fields], axis=1)
    half = line.shape[1] // 2
    lines = jnp.concatenate([line[:, :half], line[:, half:]], axis=0).astype(jnp.bfloat16)
    out_ref[...] = jnp.broadcast_to(lines[None], out_ref.shape)


def stack_kernel(
    base_ref, turn_ref, here_ref, next_ref, bank_ref, out_ref, rms_ref, rows_ref, toeplitz, normed, total,
    *, template_len, stations, block_len, bank,
):
    depth = toeplitz.shape[0]
    blocks = toeplitz.shape[1] // LANES
    out_blocks = block_len // LANES
    station_rows = bank * ROW_STEP
    half = here_ref.shape[2]
    samples = jnp.concatenate(
        [
            here_ref[:, 0, :].astype(jnp.float32),
            here_ref[:, 1, : block_len - half].astype(jnp.float32),
            next_ref[:, 0, :].astype(jnp.float32),
            next_ref[:, 1, : block_len - half].astype(jnp.float32),
            jnp.zeros((stations, LANES), jnp.float32),
        ],
        axis=1,
    )
    width = samples.shape[1]

    window = samples * samples
    energy, covered, size = None, 0, 1
    while covered < template_len:
        if template_len & size:
            moved = rolled_left(window, covered)
            energy = moved if energy is None else energy + moved
            covered = covered + size
        window = window + rolled_left(window, size)
        size = 2 * size
    rms_ref[...] = lax.rsqrt(energy / template_len + EPSILON) * (1.0 / math.sqrt(stations))

    for step in range(8):
        moved = rolled_left(samples, step)
        for block in range(width // LANES):
            row = (block * 8 + step) * stations
            rows_ref[row : row + stations, :] = moved[:, block * LANES : (block + 1) * LANES]
    normed[stations * station_rows : stations * station_rows + 16, :] = jnp.zeros((16, LANES), jnp.float32)

    @pl.loop(0, stations)
    def _(s):
        eight = jnp.concatenate(
            [rows_ref[pl.ds(block * 8 * stations + s, 8, stride=stations), :] for block in range(width // LANES)],
            axis=1,
        )
        for group in range(LANES // 16):
            pair = jnp.concatenate(
                [rolled_left(eight, 16 * group), rolled_left(eight, 16 * group + 8)], axis=0
            ).astype(jnp.bfloat16)
            for part in range(-(-depth // LANES)):
                row = part * LANES + 16 * group
                if row < depth:
                    toeplitz[row : row + 16, :] = pair[:, part * LANES : (part + blocks) * LANES]
        for column in range(blocks // 2):
            span = slice(2 * column * LANES, (2 * column + 2) * LANES)
            correlated = jnp.dot(bank_ref[...], toeplitz[:, span], preferred_element_type=jnp.float32)
            scaled = correlated * rms_ref[pl.ds(s, 1), span]
            for k in range(0, bank, 8):
                for half in range(2):
                    row = s * station_rows + k * ROW_STEP + 2 * column + half
                    normed[pl.ds(row, 8, stride=ROW_STEP), :] = scaled[k : k + 8, half * LANES : (half + 1) * LANES]

    lane = lax.broadcasted_iota(jnp.int32, (out_blocks, LANES), 1)

    @pl.loop(0, bank // 16)
    def _(pair):
        for one in range(16):
            k = pair * 16 + one
            summed = None
            for s in range(stations):
                base = base_ref[s * bank + k]
                turn = turn_ref[s * bank + k]
                picked = jnp.where(
                    lane >= LANES - turn, normed[pl.ds(base, out_blocks), :], normed[pl.ds(base + 1, out_blocks), :]
                )
                moved = pltpu.roll(picked, turn & (LANES - 1), 1)
                summed = moved if summed is None else summed + moved
            row = pair * 16 * out_blocks + (one // 8) * 8 * out_blocks + one % 8
            total[pl.ds(row, out_blocks, stride=8), :] = summed
    for k in range(0, bank, 16):
        for block in range(out_blocks):
            upper = total[k * out_blocks + 8 * block : k * out_blocks + 8 * block + 8, :]
            row = (k + 8) * out_blocks + 8 * block
            lower = total[row : row + 8, :]
            out_ref[k : k + 16, block * LANES : (block + 1) * LANES] = jnp.concatenate(
                [upper, lower], axis=0
            ).astype(jnp.bfloat16)


def shards(waveforms, templates, moveouts, channel_mask):
    block_len = waveforms.shape[1]
    bank, template_len = templates.shape
    stations = lax.axis_size("sta") * waveforms.shape[0]
    depth = -(-template_len // 16) * 16
    blocks = -(-(block_len + MOVE) // (2 * LANES)) * 2
    in_vmem = pl.BlockSpec(memory_space=pltpu.VMEM)
    in_smem = pl.BlockSpec(memory_space=pltpu.SMEM)

    packed = pl.pallas_call(
        pack_kernel,
        out_shape=jax.ShapeDtypeStruct((stations, 2, (block_len + 3 * bank) // 2), jnp.bfloat16),
        in_specs=[in_vmem] * 3,
        out_specs=in_vmem,
    )(waveforms, moveouts, channel_mask)
    here = lax.all_to_all(packed, "sta", 0, 0, tiled=True)
    count = lax.axis_size("tm")
    after = lax.ppermute(here, "tm", [(i, i - 1) for i in range(1, count)])

    here, templates = lax.optimization_barrier((here, templates))
    fields = here[:, 1, block_len - here.shape[2] :].astype(jnp.int32)
    coarse, fine, mask = jnp.split(fields, 3, axis=1)
    first = (jnp.arange(stations)[:, None] * bank + jnp.arange(bank)[None, :]) * ROW_STEP
    base = jnp.where(mask != 0, first + coarse, stations * bank * ROW_STEP).reshape(-1)
    turn = (LANES - fine).reshape(-1)
    bank_rows = jnp.pad(templates, ((0, 0), (0, depth - template_len)))

    return pl.pallas_call(
        functools.partial(
            stack_kernel, template_len=template_len, stations=stations, block_len=block_len, bank=bank
        ),
        out_shape=jax.ShapeDtypeStruct((bank, block_len), jnp.bfloat16),
        in_specs=[in_smem, in_smem, in_vmem, in_vmem, in_vmem],
        out_specs=in_vmem,
        scratch_shapes=[
            pltpu.VMEM((stations, 2 * block_len + LANES), jnp.float32),
            pltpu.VMEM((8 * stations * (2 * block_len // LANES + 1), LANES), jnp.float32),
            pltpu.VMEM((depth, blocks * LANES), jnp.bfloat16),
            pltpu.VMEM((stations * bank * ROW_STEP + 16, LANES), jnp.float32),
            pltpu.VMEM((bank * block_len // LANES, LANES), jnp.float32),
        ],
        compiler_params=pltpu.CompilerParams(vmem_limit_bytes=48 * 1024 * 1024),
    )(base, turn, here, after, bank_rows)


def solution(mesh):
    in_specs = (P("sta", "tm"), P("tpl", None), P("sta", "tpl"), P("sta", "tpl"))
    out_specs = P("tpl", "tm")
    return jax.shard_map(shards, mesh=mesh, in_specs=in_specs, out_specs=out_specs, check_vma=False)
```

```python
import functools
import math

import jax
import jax.numpy as jnp
from jax import lax
from jax.experimental import pallas as pl
from jax.experimental.pallas import tpu as pltpu
from jax.sharding import PartitionSpec as P

MOVE = 720
EPSILON = 1e-05
LANES = 128
ROW_STEP = 17


def rolled_left(x, by):
    return x if by == 0 else pltpu.roll(x, x.shape[1] - by, 1)


def pack_kernel(wave_ref, moves_ref, mask_ref, out_ref):
    moves = moves_ref[...]
    fields = (wave_ref[...].astype(jnp.float32), moves >> 7, moves & 127, mask_ref[...])
    line = jnp.concatenate([field.astype(jnp.float32) for field in fields], axis=1)
    half = line.shape[1] // 2
    lines = jnp.concatenate([line[:, :half], line[:, half:]], axis=0).astype(jnp.bfloat16)
    out_ref[...] = jnp.broadcast_to(lines[None], out_ref.shape)


def stack_kernel(
    base_ref, turn_ref, here_ref, next_ref, bank_ref, out_ref,
    rms_ref, rows_ref, toeplitz_even, toeplitz_odd, normed_even, normed_odd, total,
    *, template_len, stations, block_len, bank,
):
    depth = toeplitz_even.shape[0]
    blocks = toeplitz_even.shape[1] // LANES
    out_blocks = block_len // LANES
    half = here_ref.shape[2]
    samples = jnp.concatenate(
        [
            here_ref[:, 0, :].astype(jnp.float32),
            here_ref[:, 1, : block_len - half].astype(jnp.float32),
            next_ref[:, 0, :].astype(jnp.float32),
            next_ref[:, 1, : block_len - half].astype(jnp.float32),
            jnp.zeros((stations, LANES), jnp.float32),
        ],
        axis=1,
    )
    width = samples.shape[1]

    window = samples * samples
    energy, covered, size = None, 0, 1
    while covered < template_len:
        if template_len & size:
            moved = rolled_left(window, covered)
            energy = moved if energy is None else energy + moved
            covered = covered + size
        window = window + rolled_left(window, size)
        size = 2 * size
    rms_ref[...] = lax.rsqrt(energy / template_len + EPSILON) * (1.0 / math.sqrt(stations))

    for step in range(8):
        moved = rolled_left(samples, step)
        for block in range(width // LANES):
            row = (block * 8 + step) * stations
            rows_ref[row : row + stations, :] = moved[:, block * LANES : (block + 1) * LANES]
    for normed in (normed_even, normed_odd):
        normed[bank * ROW_STEP : bank * ROW_STEP + 16, :] = jnp.zeros((16, LANES), jnp.float32)
    total[...] = jnp.zeros_like(total)
    lane = lax.broadcasted_iota(jnp.int32, (out_blocks, LANES), 1)

    def lay_out(s, toeplitz):
        eight = jnp.concatenate(
            [rows_ref[pl.ds(block * 8 * stations + s, 8, stride=stations), :] for block in range(width // LANES)],
            axis=1,
        )
        for group in range(LANES // 16):
            pair = jnp.concatenate(
                [rolled_left(eight, 16 * group), rolled_left(eight, 16 * group + 8)], axis=0
            ).astype(jnp.bfloat16)
            for part in range(-(-depth // LANES)):
                row = part * LANES + 16 * group
                if row < depth:
                    toeplitz[row : row + 16, :] = pair[:, part * LANES : (part + blocks) * LANES]

    def correlate(s, toeplitz, normed, column):
        span = slice(2 * column * LANES, (2 * column + 2) * LANES)
        correlated = jnp.dot(bank_ref[...], toeplitz[:, span], preferred_element_type=jnp.float32)
        scaled = correlated * rms_ref[pl.ds(s, 1), span]
        for k in range(0, bank, 8):
            for one in range(2):
                row = k * ROW_STEP + 2 * column + one
                normed[pl.ds(row, 8, stride=ROW_STEP), :] = scaled[k : k + 8, one * LANES : (one + 1) * LANES]

    def add_moved(entry, normed, templates):
        for k in templates:
            base = base_ref[entry * bank + k]
            turn = turn_ref[entry * bank + k]
            picked = jnp.where(
                lane >= LANES - turn, normed[pl.ds(base, out_blocks), :], normed[pl.ds(base + 1, out_blocks), :]
            )
            rows = slice(k * out_blocks, (k + 1) * out_blocks)
            total[rows, :] = total[rows, :] + pltpu.roll(picked, turn & (LANES - 1), 1)

    def stage(s, toeplitz, normed, previous):
        columns = blocks // 2
        for column in range(columns):
            correlate(s, toeplitz, normed, column)
            add_moved(s, previous, range(bank * column // columns, bank * (column + 1) // columns))

    @pl.loop(0, stations // 2)
    def _(pair):
        lay_out(2 * pair, toeplitz_even)
        stage(2 * pair, toeplitz_even, normed_even, normed_odd)
        lay_out(2 * pair + 1, toeplitz_odd)
        stage(2 * pair + 1, toeplitz_odd, normed_odd, normed_even)

    add_moved(stations, normed_odd, range(bank))
    for k in range(0, bank, 16):
        for block in range(out_blocks):
            halves = [total[pl.ds(part * out_blocks + block, 8, stride=out_blocks), :] for part in (k, k + 8)]
            out_ref[k : k + 16, block * LANES : (block + 1) * LANES] = jnp.concatenate(halves, axis=0).astype(
                jnp.bfloat16
            )


def shards(waveforms, templates, moveouts, channel_mask):
    block_len = waveforms.shape[1]
    bank, template_len = templates.shape
    stations = lax.axis_size("sta") * waveforms.shape[0]
    depth = -(-template_len // 16) * 16
    blocks = -(-(block_len + MOVE) // (2 * LANES)) * 2
    in_vmem = pl.BlockSpec(memory_space=pltpu.VMEM)
    in_smem = pl.BlockSpec(memory_space=pltpu.SMEM)

    packed = pl.pallas_call(
        pack_kernel,
        out_shape=jax.ShapeDtypeStruct((stations, 2, (block_len + 3 * bank) // 2), jnp.bfloat16),
        in_specs=[in_vmem] * 3,
        out_specs=in_vmem,
    )(waveforms, moveouts, channel_mask)
    here = lax.all_to_all(packed, "sta", 0, 0, tiled=True)
    count = lax.axis_size("tm")
    after = lax.ppermute(here, "tm", [(i, i - 1) for i in range(1, count)])

    here, templates = lax.optimization_barrier((here, templates))
    fields = here[:, 1, block_len - here.shape[2] :].astype(jnp.int32)
    coarse, fine, mask = jnp.split(fields, 3, axis=1)
    first = jnp.arange(bank)[None, :] * ROW_STEP
    base = jnp.where(mask != 0, first + coarse, bank * ROW_STEP)
    base = jnp.pad(base, ((1, 0), (0, 0)), constant_values=bank * ROW_STEP).reshape(-1)
    turn = jnp.pad(LANES - fine, ((1, 0), (0, 0)), constant_values=LANES).reshape(-1)
    bank_rows = jnp.pad(templates, ((0, 0), (0, depth - template_len)))

    return pl.pallas_call(
        functools.partial(
            stack_kernel, template_len=template_len, stations=stations, block_len=block_len, bank=bank
        ),
        out_shape=jax.ShapeDtypeStruct((bank, block_len), jnp.bfloat16),
        in_specs=[in_smem, in_smem, in_vmem, in_vmem, in_vmem],
        out_specs=in_vmem,
        scratch_shapes=[
            pltpu.VMEM((stations, 2 * block_len + LANES), jnp.float32),
            pltpu.VMEM((8 * stations * (2 * block_len // LANES + 1), LANES), jnp.float32),
            pltpu.VMEM((depth, blocks * LANES), jnp.bfloat16),
            pltpu.VMEM((depth, blocks * LANES), jnp.bfloat16),
            pltpu.VMEM((bank * ROW_STEP + 16, LANES), jnp.float32),
            pltpu.VMEM((bank * ROW_STEP + 16, LANES), jnp.float32),
            pltpu.VMEM((bank * block_len // LANES, LANES), jnp.float32),
        ],
        compiler_params=pltpu.CompilerParams(vmem_limit_bytes=48 * 1024 * 1024),
    )(base, turn, here, after, bank_rows)


def solution(mesh):
    in_specs = (P("sta", "tm"), P("tpl", None), P("sta", "tpl"), P("sta", "tpl"))
    out_specs = P("tpl", "tm")
    return jax.shard_map(shards, mesh=mesh, in_specs=in_specs, out_specs=out_specs, check_vma=False)
```

```python
import functools
import math

import jax
import jax.numpy as jnp
from jax import lax
from jax.experimental import pallas as pl
from jax.experimental.pallas import tpu as pltpu
from jax.sharding import PartitionSpec as P

MOVE = 720
EPSILON = 1e-05
LANES = 128
ROW_STEP = 17
WIDE = 14
PIECE = 64


def rolled_left(x, by):
    return x if by == 0 else pltpu.roll(x, x.shape[1] - by, 1)


def pack_kernel(wave_hbm, moves_hbm, mask_hbm, out_ref, wave_ref, moves_ref, mask_ref, sems):
    given = ((wave_hbm, wave_ref), (moves_hbm, moves_ref), (mask_hbm, mask_ref))
    copies = [pltpu.make_async_copy(source, target, sems.at[i]) for i, (source, target) in enumerate(given)]
    for copy in copies:
        copy.start()
    for copy in copies:
        copy.wait()
    moves = moves_ref[...]
    fields = (wave_ref[...].astype(jnp.float32), moves >> 7, moves & 127, mask_ref[...])
    line = jnp.concatenate([field.astype(jnp.float32) for field in fields], axis=1)
    half = line.shape[1] // 2
    lines = jnp.concatenate([line[:, :half], line[:, half:]], axis=0).astype(jnp.bfloat16)
    out_ref[...] = jnp.broadcast_to(lines[None], out_ref.shape)


def stack_kernel(
    moves_ref, here_ref, next_ref, bank_ref, out_ref,
    places, moves_sem, stacked, out_sem, rms_ref, rows_ref, toeplitz_a, toeplitz_b, toeplitz_c, toeplitz_d, normed_a, normed_b, normed_c, normed_d, total,
    *, template_len, stations, block_len, bank,
):
    depth = toeplitz_a.shape[0]
    blocks = toeplitz_a.shape[1] // LANES
    out_blocks = block_len // LANES
    half = here_ref.shape[2]
    fetch = pltpu.make_async_copy(moves_ref, places, moves_sem)
    fetch.start()
    samples = jnp.concatenate(
        [
            here_ref[:, 0, :].astype(jnp.float32),
            here_ref[:, 1, : block_len - half].astype(jnp.float32),
            next_ref[:, 0, :].astype(jnp.float32),
            next_ref[:, 1, : block_len - half].astype(jnp.float32),
            jnp.zeros((stations, LANES), jnp.float32),
        ],
        axis=1,
    )
    width = samples.shape[1]

    window = samples * samples
    energy, covered, size = None, 0, 1
    while covered < template_len:
        if template_len & size:
            moved = rolled_left(window, covered)
            energy = moved if energy is None else energy + moved
            covered = covered + size
        window = window + rolled_left(window, size)
        size = 2 * size
    rms_ref[...] = lax.rsqrt(energy / template_len + EPSILON) * (1.0 / math.sqrt(stations))

    for step in range(8):
        moved = rolled_left(samples, step)
        for block in range(width // LANES):
            row = (block * 8 + step) * stations
            rows_ref[row : row + stations, :] = moved[:, block * LANES : (block + 1) * LANES]
    for normed in (normed_a, normed_b, normed_c, normed_d):
        normed[bank * ROW_STEP : bank * ROW_STEP + 16, :] = jnp.zeros((16, LANES), jnp.float32)
    lane = lax.broadcasted_iota(jnp.int32, (out_blocks, LANES), 1)

    def lay_out(s, group, toeplitz):
        eight = jnp.concatenate(
            [rows_ref[pl.ds(block * 8 * stations + s, 8, stride=stations), :] for block in range(width // LANES)],
            axis=1,
        )
        pair = jnp.concatenate(
            [rolled_left(eight, 16 * group), rolled_left(eight, 16 * group + 8)], axis=0
        ).astype(jnp.bfloat16)
        for part in range(-(-depth // LANES)):
            row = part * LANES + 16 * group
            if row < depth:
                toeplitz[row : row + 16, :] = pair[:, part * LANES : (part + blocks) * LANES]

    def correlate(s, toeplitz, normed, first, last):
        span = slice(first * LANES, last * LANES)
        correlated = jnp.dot(bank_ref[...], toeplitz[:, span], preferred_element_type=jnp.float32)
        scaled = correlated * rms_ref[s : s + 1, span]
        for k in range(0, bank, 8):
            for block in range(first, last):
                row = k * ROW_STEP + block
                column = (block - first) * LANES
                normed[pl.ds(row, 8, stride=ROW_STEP), :] = scaled[k : k + 8, column : column + LANES]

    def add_moved(members, buffers, templates):
        for k in templates:
            rows = slice(k * out_blocks, (k + 1) * out_blocks)
            summed = None if members[0] == 0 else total[rows, :]
            for s, normed in zip(members, buffers):
                base = places[s * bank + k]
                turn = places[(stations + s) * bank + k]
                picked = jnp.where(
                    lane >= LANES - turn, normed[pl.ds(base, out_blocks), :], normed[pl.ds(base + 1, out_blocks), :]
                )
                moved = pltpu.roll(picked, turn & (LANES - 1), 1)
                summed = moved if summed is None else summed + moved
            total[rows, :] = summed

    toeplitz = ((toeplitz_a, toeplitz_b), (toeplitz_c, toeplitz_d))
    normed = ((normed_a, normed_b), (normed_c, normed_d))
    members = [(s, s + 1) for s in range(0, stations - 2, 2)] + [(stations - 2,), (stations - 1,)]
    spans = [(first, min(first + WIDE, blocks)) for first in range(0, blocks, WIDE)]
    groups = LANES // 16

    def stage(p):
        jobs = [(one, span) for span in spans for one in range(len(members[p]))]
        for j, (one, span) in enumerate(jobs):
            share = lambda amount: range(amount * j // len(jobs), amount * (j + 1) // len(jobs))
            correlate(members[p][one], toeplitz[p % 2][one], normed[p % 2][one], *span)
            if p + 1 < len(members):
                for step in share(len(members[p + 1]) * groups):
                    lay_out(members[p + 1][step // groups], step % groups, toeplitz[(p + 1) % 2][step // groups])
            if p > 0:
                add_moved(members[p - 1], normed[(p - 1) % 2], share(bank))

    for one in range(2):
        for group in range(groups):
            lay_out(members[0][one], group, toeplitz[0][one])
    fetch.wait()
    for p in range(len(members)):
        stage(p)
    writes = []
    for first in range(0, bank, PIECE):
        add_moved(members[-1], normed[(len(members) - 1) % 2], range(first, first + PIECE))
        for k in range(first, first + PIECE, 16):
            for block in range(out_blocks):
                halves = [total[pl.ds(part * out_blocks + block, 8, stride=out_blocks), :] for part in (k, k + 8)]
                stacked[k : k + 16, block * LANES : (block + 1) * LANES] = jnp.concatenate(halves, axis=0).astype(
                    jnp.bfloat16
                )
        piece = pl.ds(first, PIECE)
        writes.append(pltpu.make_async_copy(stacked.at[piece], out_ref.at[piece], out_sem.at[first // PIECE]))
        writes[-1].start()
    for write in writes:
        write.wait()


def shards(waveforms, templates, moveouts, channel_mask):
    block_len = waveforms.shape[1]
    bank, template_len = templates.shape
    stations = lax.axis_size("sta") * waveforms.shape[0]
    depth = -(-template_len // 16) * 16
    blocks = -(-(block_len + MOVE) // (2 * LANES)) * 2
    in_vmem = pl.BlockSpec(memory_space=pltpu.VMEM)

    packed = pl.pallas_call(
        pack_kernel,
        out_shape=jax.ShapeDtypeStruct((stations, 2, (block_len + 3 * bank) // 2), jnp.bfloat16),
        in_specs=[pl.BlockSpec(memory_space=pltpu.HBM)] * 3,
        out_specs=in_vmem,
        scratch_shapes=[
            *[pltpu.VMEM(given.shape, given.dtype) for given in (waveforms, moveouts, channel_mask)],
            pltpu.SemaphoreType.DMA((3,)),
        ],
    )(waveforms, moveouts, channel_mask)
    here = lax.all_to_all(packed, "sta", 0, 0, tiled=True)
    count = lax.axis_size("tm")
    after = lax.ppermute(here, "tm", [(i, i - 1) for i in range(1, count)])

    here, templates = lax.optimization_barrier((here, templates))
    fields = here[:, 1, block_len - here.shape[2] :].astype(jnp.int32)
    coarse, fine, mask = jnp.split(fields, 3, axis=1)
    first = jnp.arange(bank)[None, :] * ROW_STEP
    base = jnp.where(mask != 0, first + coarse, bank * ROW_STEP)
    places = jnp.concatenate([base, LANES - fine], axis=0).reshape(-1)
    bank_rows = jnp.pad(templates, ((0, 0), (0, depth - template_len)))

    return pl.pallas_call(
        functools.partial(
            stack_kernel, template_len=template_len, stations=stations, block_len=block_len, bank=bank
        ),
        out_shape=jax.ShapeDtypeStruct((bank, block_len), jnp.bfloat16),
        in_specs=[in_vmem] * 4,
        out_specs=pl.BlockSpec(memory_space=pl.ANY),
        scratch_shapes=[
            pltpu.SMEM((2 * stations * bank,), jnp.int32),
            pltpu.SemaphoreType.DMA,
            pltpu.VMEM((bank, block_len), jnp.bfloat16),
            pltpu.SemaphoreType.DMA((bank // PIECE,)),
            pltpu.VMEM((stations, 2 * block_len + LANES), jnp.float32),
            pltpu.VMEM((8 * stations * (2 * block_len // LANES + 1), LANES), jnp.float32),
            *[pltpu.VMEM((depth, blocks * LANES), jnp.bfloat16)] * 4,
            *[pltpu.VMEM((bank * ROW_STEP + 16, LANES), jnp.float32)] * 4,
            pltpu.VMEM((bank * block_len // LANES, LANES), jnp.float32),
        ],
        compiler_params=pltpu.CompilerParams(vmem_limit_bytes=48 * 1024 * 1024),
    )(places, here, after, bank_rows)


def solution(mesh):
    in_specs = (P("sta", "tm"), P("tpl", None), P("sta", "tpl"), P("sta", "tpl"))
    out_specs = P("tpl", "tm")
    return jax.shard_map(shards, mesh=mesh, in_specs=in_specs, out_specs=out_specs, check_vma=False)
```

```python
import functools
import math

import jax
import jax.numpy as jnp
from jax import lax
from jax.experimental import pallas as pl
from jax.experimental.pallas import tpu as pltpu
from jax.sharding import PartitionSpec as P

MOVE = 720
EPSILON = 1e-05
LANES = 128
ROW_STEP = 17
WIDE = 14
PIECE = 64


def rolled_left(x, by):
    return x if by == 0 else pltpu.roll(x, x.shape[1] - by, 1)


def pack_kernel(known_ref, after_ref, out_ref):
    block_len = after_ref.shape[1]
    fields = (known_ref[:, :block_len], after_ref[...], known_ref[:, block_len:])
    line = jnp.concatenate([field.astype(jnp.float32) for field in fields], axis=1)
    half = line.shape[1] // 2
    lines = jnp.concatenate([line[:, :half], line[:, half:]], axis=0).astype(jnp.bfloat16)
    out_ref[...] = jnp.broadcast_to(lines[None], out_ref.shape)


def stack_kernel(
    moves_ref, here_ref, bank_ref, out_ref,
    places, moves_sem, stacked, out_sem, rms_ref, rows_ref, toeplitz_a, toeplitz_b, toeplitz_c, toeplitz_d, normed_a, normed_b, normed_c, normed_d, total,
    *, template_len, stations, block_len, bank,
):
    depth = toeplitz_a.shape[0]
    blocks = toeplitz_a.shape[1] // LANES
    out_blocks = block_len // LANES
    half = here_ref.shape[2]
    fetch = pltpu.make_async_copy(moves_ref, places, moves_sem)
    fetch.start()
    samples = jnp.concatenate(
        [
            here_ref[:, 0, :].astype(jnp.float32),
            here_ref[:, 1, : 2 * block_len - half].astype(jnp.float32),
            jnp.zeros((stations, LANES), jnp.float32),
        ],
        axis=1,
    )
    width = samples.shape[1]

    window = samples * samples
    energy, covered, size = None, 0, 1
    while covered < template_len:
        if template_len & size:
            moved = rolled_left(window, covered)
            energy = moved if energy is None else energy + moved
            covered = covered + size
        window = window + rolled_left(window, size)
        size = 2 * size
    rms_ref[...] = lax.rsqrt(energy / template_len + EPSILON) * (1.0 / math.sqrt(stations))

    for step in range(8):
        moved = rolled_left(samples, step)
        for block in range(width // LANES):
            row = (block * 8 + step) * stations
            rows_ref[row : row + stations, :] = moved[:, block * LANES : (block + 1) * LANES]
    for normed in (normed_a, normed_b, normed_c, normed_d):
        normed[bank * ROW_STEP : bank * ROW_STEP + 16, :] = jnp.zeros((16, LANES), jnp.float32)
    lane = lax.broadcasted_iota(jnp.int32, (out_blocks, LANES), 1)

    def lay_out(s, group, toeplitz):
        eight = jnp.concatenate(
            [rows_ref[pl.ds(block * 8 * stations + s, 8, stride=stations), :] for block in range(width // LANES)],
            axis=1,
        )
        pair = jnp.concatenate(
            [rolled_left(eight, 16 * group), rolled_left(eight, 16 * group + 8)], axis=0
        ).astype(jnp.bfloat16)
        for part in range(-(-depth // LANES)):
            row = part * LANES + 16 * group
            if row < depth:
                toeplitz[row : row + 16, :] = pair[:, part * LANES : (part + blocks) * LANES]

    def correlate(s, toeplitz, normed, first, last):
        span = slice(first * LANES, last * LANES)
        correlated = jnp.dot(bank_ref[...], toeplitz[:, span], preferred_element_type=jnp.float32)
        scaled = correlated * rms_ref[s : s + 1, span]
        for k in range(0, bank, 8):
            for block in range(first, last):
                row = k * ROW_STEP + block
                column = (block - first) * LANES
                normed[pl.ds(row, 8, stride=ROW_STEP), :] = scaled[k : k + 8, column : column + LANES]

    def add_moved(members, buffers, templates):
        for k in templates:
            rows = slice(k * out_blocks, (k + 1) * out_blocks)
            summed = None if members[0] == 0 else total[rows, :]
            for s, normed in zip(members, buffers):
                base = places[s * bank + k]
                turn = places[(stations + s) * bank + k]
                picked = jnp.where(
                    lane >= LANES - turn, normed[pl.ds(base, out_blocks), :], normed[pl.ds(base + 1, out_blocks), :]
                )
                moved = pltpu.roll(picked, turn & (LANES - 1), 1)
                summed = moved if summed is None else summed + moved
            total[rows, :] = summed

    toeplitz = ((toeplitz_a, toeplitz_b), (toeplitz_c, toeplitz_d))
    normed = ((normed_a, normed_b), (normed_c, normed_d))
    members = [(s, s + 1) for s in range(0, stations - 2, 2)] + [(stations - 2,), (stations - 1,)]
    spans = [(first, min(first + WIDE, blocks)) for first in range(0, blocks, WIDE)]
    groups = LANES // 16

    def stage(p):
        jobs = [(one, span) for span in spans for one in range(len(members[p]))]
        for j, (one, span) in enumerate(jobs):
            share = lambda amount: range(amount * j // len(jobs), amount * (j + 1) // len(jobs))
            correlate(members[p][one], toeplitz[p % 2][one], normed[p % 2][one], *span)
            if p + 1 < len(members):
                for step in share(len(members[p + 1]) * groups):
                    lay_out(members[p + 1][step // groups], step % groups, toeplitz[(p + 1) % 2][step // groups])
            if p > 0:
                add_moved(members[p - 1], normed[(p - 1) % 2], share(bank))

    for one in range(2):
        for group in range(groups):
            lay_out(members[0][one], group, toeplitz[0][one])
    fetch.wait()
    for p in range(len(members)):
        stage(p)
    writes = []
    for first in range(0, bank, PIECE):
        add_moved(members[-1], normed[(len(members) - 1) % 2], range(first, first + PIECE))
        for k in range(first, first + PIECE, 16):
            for block in range(out_blocks):
                halves = [total[pl.ds(part * out_blocks + block, 8, stride=out_blocks), :] for part in (k, k + 8)]
                stacked[k : k + 16, block * LANES : (block + 1) * LANES] = jnp.concatenate(halves, axis=0).astype(
                    jnp.bfloat16
                )
        piece = pl.ds(first, PIECE)
        writes.append(pltpu.make_async_copy(stacked.at[piece], out_ref.at[piece], out_sem.at[first // PIECE]))
        writes[-1].start()
    for write in writes:
        write.wait()


def shards(waveforms, templates, moveouts, channel_mask):
    block_len = waveforms.shape[1]
    bank, template_len = templates.shape
    stations = lax.axis_size("sta") * waveforms.shape[0]
    depth = -(-template_len // 16) * 16
    blocks = -(-(block_len + MOVE) // (2 * LANES)) * 2
    in_vmem = pl.BlockSpec(memory_space=pltpu.VMEM)

    count = lax.axis_size("tm")
    after = lax.ppermute(waveforms, "tm", [(i, i - 1) for i in range(1, count)])
    fields = (waveforms, moveouts >> 7, moveouts & 127, channel_mask)
    known = jnp.concatenate([field.astype(jnp.bfloat16) for field in fields], axis=1)
    packed = pl.pallas_call(
        pack_kernel,
        out_shape=jax.ShapeDtypeStruct((stations, 2, (2 * block_len + 3 * bank) // 2), jnp.bfloat16),
        in_specs=[in_vmem] * 2,
        out_specs=in_vmem,
        compiler_params=pltpu.CompilerParams(vmem_limit_bytes=1024 * 1024),
    )(known, after)
    here = lax.all_to_all(packed, "sta", 0, 0, tiled=True)
    fields = here[:, 1, 2 * block_len - here.shape[2] :].astype(jnp.int32)
    coarse, fine, mask = jnp.split(fields, 3, axis=1)
    first = jnp.arange(bank)[None, :] * ROW_STEP
    base = jnp.where(mask != 0, first + coarse, bank * ROW_STEP)
    places = jnp.concatenate([base, LANES - fine], axis=0).reshape(-1)
    bank_rows = jnp.pad(templates, ((0, 0), (0, depth - template_len)))

    return pl.pallas_call(
        functools.partial(
            stack_kernel, template_len=template_len, stations=stations, block_len=block_len, bank=bank
        ),
        out_shape=jax.ShapeDtypeStruct((bank, block_len), jnp.bfloat16),
        in_specs=[in_vmem] * 3,
        out_specs=pl.BlockSpec(memory_space=pl.ANY),
        scratch_shapes=[
            pltpu.SMEM((2 * stations * bank,), jnp.int32),
            pltpu.SemaphoreType.DMA,
            pltpu.VMEM((bank, block_len), jnp.bfloat16),
            pltpu.SemaphoreType.DMA((bank // PIECE,)),
            pltpu.VMEM((stations, 2 * block_len + LANES), jnp.float32),
            pltpu.VMEM((8 * stations * (2 * block_len // LANES + 1), LANES), jnp.float32),
            *[pltpu.VMEM((depth, blocks * LANES), jnp.bfloat16)] * 4,
            *[pltpu.VMEM((bank * ROW_STEP + 16, LANES), jnp.float32)] * 4,
            pltpu.VMEM((bank * block_len // LANES, LANES), jnp.float32),
        ],
        compiler_params=pltpu.CompilerParams(vmem_limit_bytes=48 * 1024 * 1024),
    )(places, here, bank_rows)


def solution(mesh):
    in_specs = (P("sta", "tm"), P("tpl", None), P("sta", "tpl"), P("sta", "tpl"))
    out_specs = P("tpl", "tm")
    return jax.shard_map(shards, mesh=mesh, in_specs=in_specs, out_specs=out_specs, check_vma=False)
```

```python
import functools
import math

import jax
import jax.numpy as jnp
from jax import lax
from jax.experimental import pallas as pl
from jax.experimental.pallas import tpu as pltpu
from jax.sharding import PartitionSpec as P

MOVE = 720
EPSILON = 1e-05
LANES = 128
ROW_STEP = 17
PIECE = 64


def rolled_left(x, by):
    return x if by == 0 else pltpu.roll(x, x.shape[1] - by, 1)


def pack_kernel(known_ref, after_ref, out_ref):
    block_len = after_ref.shape[1]
    fields = (known_ref[:, :block_len], after_ref[...], known_ref[:, block_len:])
    line = jnp.concatenate([field.astype(jnp.float32) for field in fields], axis=1)
    half = line.shape[1] // 2
    lines = jnp.concatenate([line[:, :half], line[:, half:]], axis=0).astype(jnp.bfloat16)
    out_ref[...] = jnp.broadcast_to(lines[None], out_ref.shape)


def stack_kernel(
    moves_ref, here_ref, bank_ref, out_ref,
    places, moves_sem, stacked, out_sem, rms_ref, rows_ref, toeplitz_a, toeplitz_b, toeplitz_c, toeplitz_d, normed_a, normed_b, normed_c, normed_d, total,
    *, template_len, stations, block_len, bank,
):
    depth = toeplitz_a.shape[0]
    blocks = toeplitz_a.shape[1] // LANES
    out_blocks = block_len // LANES
    half = here_ref.shape[2]
    fetch = pltpu.make_async_copy(moves_ref, places, moves_sem)
    fetch.start()
    samples = jnp.concatenate(
        [
            here_ref[:, 0, :].astype(jnp.float32),
            here_ref[:, 1, : 2 * block_len - half].astype(jnp.float32),
            jnp.zeros((stations, LANES), jnp.float32),
        ],
        axis=1,
    )
    width = samples.shape[1]

    window = samples * samples
    energy, covered, size = None, 0, 1
    while covered < template_len:
        if template_len & size:
            moved = rolled_left(window, covered)
            energy = moved if energy is None else energy + moved
            covered = covered + size
        window = window + rolled_left(window, size)
        size = 2 * size
    rms_ref[...] = lax.rsqrt(energy / template_len + EPSILON) * (1.0 / math.sqrt(stations))

    for step in range(8):
        moved = rolled_left(samples, step)
        for block in range(width // LANES):
            row = (block * 8 + step) * stations
            rows_ref[row : row + stations, :] = moved[:, block * LANES : (block + 1) * LANES]
    for normed in (normed_a, normed_b, normed_c, normed_d):
        normed[bank * ROW_STEP : bank * ROW_STEP + 16, :] = jnp.zeros((16, LANES), jnp.float32)
    lane = lax.broadcasted_iota(jnp.int32, (out_blocks, LANES), 1)

    def lay_out(s, group, toeplitz):
        eight = jnp.concatenate(
            [rows_ref[pl.ds(block * 8 * stations + s, 8, stride=stations), :] for block in range(width // LANES)],
            axis=1,
        )
        pair = jnp.concatenate(
            [rolled_left(eight, 16 * group), rolled_left(eight, 16 * group + 8)], axis=0
        ).astype(jnp.bfloat16)
        for part in range(-(-depth // LANES)):
            row = part * LANES + 16 * group
            if row < depth:
                toeplitz[row : row + 16, :] = pair[:, part * LANES : (part + blocks) * LANES]

    def correlate(members, toeplitz, normed):
        taps = jnp.concatenate([one[...] for one in toeplitz[: len(members)]], axis=1)
        rms = jnp.concatenate([rms_ref[s : s + 1, : blocks * LANES] for s in members], axis=1)
        scaled = jnp.dot(bank_ref[...], taps, preferred_element_type=jnp.float32) * rms
        for one in range(len(members)):
            for k in range(0, bank, 8):
                for block in range(blocks):
                    column = (one * blocks + block) * LANES
                    normed[one][pl.ds(k * ROW_STEP + block, 8, stride=ROW_STEP), :] = scaled[
                        k : k + 8, column : column + LANES
                    ]

    def add_moved(members, buffers, templates):
        for k in templates:
            rows = slice(k * out_blocks, (k + 1) * out_blocks)
            summed = None if members[0] == 0 else total[rows, :]
            for s, normed in zip(members, buffers):
                base = places[s * bank + k]
                turn = places[(stations + s) * bank + k]
                picked = jnp.where(
                    lane >= LANES - turn, normed[pl.ds(base, out_blocks), :], normed[pl.ds(base + 1, out_blocks), :]
                )
                moved = pltpu.roll(picked, turn & (LANES - 1), 1)
                summed = moved if summed is None else summed + moved
            total[rows, :] = summed

    toeplitz = ((toeplitz_a, toeplitz_b), (toeplitz_c, toeplitz_d))
    normed = ((normed_a, normed_b), (normed_c, normed_d))
    members = [(s, s + 1) for s in range(0, stations, 2)]
    groups = LANES // 16

    def stage(p):
        correlate(members[p], toeplitz[p % 2], normed[p % 2])
        if p + 1 < len(members):
            for one, s in enumerate(members[p + 1]):
                for group in range(groups):
                    lay_out(s, group, toeplitz[(p + 1) % 2][one])
        if p > 0:
            add_moved(members[p - 1], normed[(p - 1) % 2], range(bank))

    for one in range(2):
        for group in range(groups):
            lay_out(members[0][one], group, toeplitz[0][one])
    fetch.wait()
    for p in range(len(members)):
        stage(p)
    writes = []
    for first in range(0, bank, PIECE):
        add_moved(members[-1], normed[(len(members) - 1) % 2], range(first, first + PIECE))
        for k in range(first, first + PIECE, 16):
            for block in range(out_blocks):
                halves = [total[pl.ds(part * out_blocks + block, 8, stride=out_blocks), :] for part in (k, k + 8)]
                stacked[k : k + 16, block * LANES : (block + 1) * LANES] = jnp.concatenate(halves, axis=0).astype(
                    jnp.bfloat16
                )
        piece = pl.ds(first, PIECE)
        writes.append(pltpu.make_async_copy(stacked.at[piece], out_ref.at[piece], out_sem.at[first // PIECE]))
        writes[-1].start()
    for write in writes:
        write.wait()


def shards(waveforms, templates, moveouts, channel_mask):
    block_len = waveforms.shape[1]
    bank, template_len = templates.shape
    stations = lax.axis_size("sta") * waveforms.shape[0]
    depth = -(-template_len // 16) * 16
    blocks = -(-(block_len + MOVE) // (2 * LANES)) * 2
    in_vmem = pl.BlockSpec(memory_space=pltpu.VMEM)

    count = lax.axis_size("tm")
    after = lax.ppermute(waveforms, "tm", [(i, i - 1) for i in range(1, count)])
    fields = (waveforms, moveouts >> 7, moveouts & 127, channel_mask)
    known = jnp.concatenate([field.astype(jnp.bfloat16) for field in fields], axis=1)
    packed = pl.pallas_call(
        pack_kernel,
        out_shape=jax.ShapeDtypeStruct((stations, 2, (2 * block_len + 3 * bank) // 2), jnp.bfloat16),
        in_specs=[in_vmem] * 2,
        out_specs=in_vmem,
        compiler_params=pltpu.CompilerParams(vmem_limit_bytes=1024 * 1024),
    )(known, after)
    here = lax.all_to_all(packed, "sta", 0, 0, tiled=True)
    fields = here[:, 1, 2 * block_len - here.shape[2] :].astype(jnp.int32)
    coarse, fine, mask = jnp.split(fields, 3, axis=1)
    first = jnp.arange(bank)[None, :] * ROW_STEP
    base = jnp.where(mask != 0, first + coarse, bank * ROW_STEP)
    places = jnp.concatenate([base, LANES - fine], axis=0).reshape(-1)
    bank_rows = jnp.pad(templates, ((0, 0), (0, depth - template_len)))

    return pl.pallas_call(
        functools.partial(
            stack_kernel, template_len=template_len, stations=stations, block_len=block_len, bank=bank
        ),
        out_shape=jax.ShapeDtypeStruct((bank, block_len), jnp.bfloat16),
        in_specs=[in_vmem] * 3,
        out_specs=pl.BlockSpec(memory_space=pl.ANY),
        scratch_shapes=[
            pltpu.SMEM((2 * stations * bank,), jnp.int32),
            pltpu.SemaphoreType.DMA,
            pltpu.VMEM((bank, block_len), jnp.bfloat16),
            pltpu.SemaphoreType.DMA((bank // PIECE,)),
            pltpu.VMEM((stations, 2 * block_len + LANES), jnp.float32),
            pltpu.VMEM((8 * stations * (2 * block_len // LANES + 1), LANES), jnp.float32),
            *[pltpu.VMEM((depth, blocks * LANES), jnp.bfloat16)] * 4,
            *[pltpu.VMEM((bank * ROW_STEP + 16, LANES), jnp.float32)] * 4,
            pltpu.VMEM((bank * block_len // LANES, LANES), jnp.float32),
        ],
        compiler_params=pltpu.CompilerParams(vmem_limit_bytes=48 * 1024 * 1024),
    )(places, here, bank_rows)


def solution(mesh):
    in_specs = (P("sta", "tm"), P("tpl", None), P("sta", "tpl"), P("sta", "tpl"))
    out_specs = P("tpl", "tm")
    return jax.shard_map(shards, mesh=mesh, in_specs=in_specs, out_specs=out_specs, check_vma=False)
```
